256 devices in a mesh: req: 4 (over x), pos: 64 (over y, z, core).
Axes of the slice: x: 4, y: 4, z: 8, core: 2. Of those that a mesh axis runs over, the one named last changes fastest.
Arguments:
- hidden: bfloat16 [2048, 8192], P(('req', 'pos')), parts along dimension 0, may hold values from -6 to 6
- norm_gain: bfloat16 [8192], replicated, may hold values from 0.099609375 to 1.8984375
- w_query: bfloat16 [8192, 4096], P('pos'), may hold values from -0.0625 to 0.0625
- key_weight: bfloat16 [8192, 512], P('pos'), may hold values from -0.0625 to 0.0625
- value_weight: bfloat16 [8192, 512], P('pos'), may hold values from -0.0625 to 0.0625
- rotated_key_cache: bfloat16 [512, 128, 512], P(('req', 'pos')), parts along dimension 0
- paged_value_cache: bfloat16 [512, 128, 512], P(('req', 'pos')), parts along dimension 0, may hold values from -6 to 6
- page_map: int32 [512], P(('req', 'pos')), parts along dimension 0, may hold values from 0 to 127, each once
- selected_positions: int32 [2048], P('req'), parts along dimension 0, may hold values from 0 to 16383, as said below
Outputs:
- blended: bfloat16 [2048, 4096], P(('req', 'pos')), parts along dimension 0
- new_key_cache: bfloat16 [512, 128, 512], P(('req', 'pos')), parts along dimension 0
- new_value_cache: bfloat16 [512, 128, 512], P(('req', 'pos')), parts along dimension 0
The draws below stay inside these ranges and needn't reach their ends.
There are 4 independent parts, one for each index of `req`. The reference program is written for one: setup_inputs(seed, part) draws one part's arguments, and reference() takes and returns one part's arrays. A program takes and returns all parts, laid end to end along the dimension named above; an argument that names none is the same for every part. Nothing has to cross between parts.
Inputs may be any that keep to these rules, and one draw needn't show every extreme that they name: `selected_positions`: 512 distinct positions in increasing order, all below the length of the request, which is a whole number between 5 and 16 of documents of 1024 tokens; the first and the last position of the request are always selected, and some request has 16 documents.
All inputs are finite; a program needn't handle non-finite values.
Results may differ from the reference program's by a relative error of at most 0.015.
The reference program's roundings to bfloat16 on the way count: a program that leaves them out, or rounds other values in their place, can miss the bound.
Values may be sent and summed in bfloat16 or wider, within the bound.
No kernel may reach another device: no remote copies, remote signals or barrier semaphores. Data moves between devices by JAX's collectives and lax.ppermute only.
A program may use at most 128 MiB of HBM per device.

```python
import jax
import jax.numpy as jnp
from jax import lax

MODEL_WIDTH = 8192
QUERY_HEADS = 32
KEY_VALUE_HEADS = 4
HEAD_SIZE = 128
PAGE_TOKENS = 128
DOC_LEN = 1024
PAGES_DEV = 2
SELECTED_TOKENS = 512
REQUEST_PAGES = 128
MAXDOC = 16
MINDOC = 5
N_POS = 64


def draw_rotated_key_cache(key, part):
    key = jax.random.fold_in(key, 11)
    first = jax.random.fold_in(key, 0)
    target_shape = (REQUEST_PAGES, PAGE_TOKENS, KEY_VALUE_HEADS * HEAD_SIZE)
    return jnp.clip(jax.random.normal(first, target_shape, jnp.float32), -6.0, 6.0).astype(jnp.bfloat16)


def draw_selected_positions(key, part):
    key = jax.random.fold_in(key, 7)
    first, second = jax.random.split(key)
    drawn = jax.random.randint(first, (), MINDOC, MAXDOC + 1)
    documents = jnp.where(part == 0, MAXDOC, drawn)
    length = documents * DOC_LEN
    places = jnp.arange(REQUEST_PAGES * PAGE_TOKENS, dtype=jnp.int32)
    shuffled = jax.random.permutation(second, REQUEST_PAGES * PAGE_TOKENS).astype(jnp.int32)
    ranked = jnp.where(places < length, shuffled, -1)
    ranked = jnp.where(places == length - 1, REQUEST_PAGES * PAGE_TOKENS, ranked)
    ranked = jnp.where(places == 0, REQUEST_PAGES * PAGE_TOKENS + 1, ranked)
    _, picked = jax.lax.top_k(ranked, SELECTED_TOKENS)
    return jnp.sort(picked.astype(jnp.int32))


def steps_of(key, extent, shards, smallest, top_value):
    def one(axis_at, shards_of):
        draws = jax.random.uniform(jax.random.fold_in(jax.random.fold_in(key, 6), axis_at), (shards_of,), jnp.float32, smallest / len(shards), top_value / len(shards))
        return jnp.repeat(jnp.exp(draws), extent[axis_at] // shards_of).reshape((-1,) + (1,) * (len(extent) - axis_at - 1))

    factor_of = one(*shards[0])
    for cut in shards[1:]:
        factor_of = factor_of * one(*cut)
    return factor_of


def noise(key, shape, deviation, bound, cuts=(), held_as=jnp.bfloat16):
    array = jax.random.normal(key, shape, jnp.float32) * deviation
    if len(cuts) > 0:
        array = steps_of(key, shape, cuts, -0.22, 0.18) * array
    return jnp.clip(array, min=-bound, max=bound).astype(held_as)


def setup_inputs(seed: int = 0, part: int = 0) -> dict:
    arg_keys = jax.random.split(jax.random.key(seed), 10)
    own_keys = jax.random.split(jax.random.fold_in(arg_keys[9], part), 10)
    hidden = noise(own_keys[0], (SELECTED_TOKENS, MODEL_WIDTH), 1.0, 6.0, ((0, 64),))
    norm_gain = jnp.clip(1.0 + 0.18 * jax.random.normal(arg_keys[1], (MODEL_WIDTH,), jnp.float32), 0.099609375, 1.8984375).astype(jnp.bfloat16)
    w_query = noise(arg_keys[2], (MODEL_WIDTH, QUERY_HEADS * HEAD_SIZE), MODEL_WIDTH ** -0.5, 0.0625, ((0, 64),))
    key_weight = noise(arg_keys[3], (MODEL_WIDTH, KEY_VALUE_HEADS * HEAD_SIZE), MODEL_WIDTH ** -0.5, 0.0625, ((0, 64),))
    value_weight = noise(arg_keys[4], (MODEL_WIDTH, KEY_VALUE_HEADS * HEAD_SIZE), MODEL_WIDTH ** -0.5, 0.0625, ((0, 64),))
    rotated_key_cache = draw_rotated_key_cache(jax.random.fold_in(jax.random.fold_in(arg_keys[9], part), 71), part)
    paged_value_cache = noise(own_keys[6], (REQUEST_PAGES, PAGE_TOKENS, KEY_VALUE_HEADS * HEAD_SIZE), 1.0, 6.0, ((0, 64),))
    page_map = jax.random.permutation(own_keys[7], REQUEST_PAGES).astype(jnp.int32)
    selected_positions = draw_selected_positions(jax.random.fold_in(jax.random.fold_in(arg_keys[9], part), 71), part)
    return dict(hidden=hidden, norm_gain=norm_gain, w_query=w_query, key_weight=key_weight, value_weight=value_weight, rotated_key_cache=rotated_key_cache, paged_value_cache=paged_value_cache, page_map=page_map, selected_positions=selected_positions)


def apply_rotation(values, positions, heads):
    count = values.shape[0]
    width = values.shape[1] // heads
    half = width // 2
    shaped = values.reshape(count, heads, width)
    frequency = 500000.0 ** (-(jnp.arange(half, dtype=jnp.float32) * 2.0 / width))
    angles = positions.astype(jnp.float32)[:, None] * frequency[None, :]
    cosine = jnp.cos(angles)[:, None, :]
    sine = jnp.sin(angles)[:, None, :]
    first = shaped[..., :half]
    second = shaped[..., half:]
    joined = jnp.concatenate([first * cosine - second * sine, second * cosine + first * sine], axis=-1)
    return joined.reshape(count, heads * width)

def reference(hidden, norm_gain, w_query, key_weight, value_weight, rotated_key_cache, paged_value_cache, page_map, selected_positions):
    values = hidden.astype(jnp.float32)
    meansq = lax.optimization_barrier(jnp.mean(values * values, axis=-1, keepdims=True))
    normalized_rows = (values * lax.rsqrt(meansq + 1e-05) * norm_gain.astype(jnp.float32)).astype(jnp.bfloat16)
    query_rows = apply_rotation(jnp.dot(normalized_rows, w_query, preferred_element_type=jnp.float32), selected_positions, QUERY_HEADS).astype(jnp.bfloat16)
    recomputed_key = apply_rotation(jnp.dot(normalized_rows, key_weight, preferred_element_type=jnp.float32), selected_positions, KEY_VALUE_HEADS).astype(jnp.bfloat16)
    recomputed_value = jnp.dot(normalized_rows, value_weight, preferred_element_type=jnp.float32).astype(jnp.bfloat16)
    inverse = jnp.zeros((REQUEST_PAGES,), jnp.int32).at[page_map].set(jnp.arange(REQUEST_PAGES, dtype=jnp.int32))
    target_slots = (inverse[selected_positions // PAGE_TOKENS] * PAGE_TOKENS + selected_positions % PAGE_TOKENS).astype(jnp.int32)
    key_flattened = rotated_key_cache.reshape(REQUEST_PAGES * PAGE_TOKENS, KEY_VALUE_HEADS * HEAD_SIZE).at[target_slots].set(recomputed_key)
    value_flattened = paged_value_cache.reshape(REQUEST_PAGES * PAGE_TOKENS, KEY_VALUE_HEADS * HEAD_SIZE).at[target_slots].set(recomputed_value)
    key_pos = (page_map[:, None] * PAGE_TOKENS + jnp.arange(PAGE_TOKENS, dtype=jnp.int32)[None, :]).reshape(-1)
    group_size = QUERY_HEADS // KEY_VALUE_HEADS
    block_index = PAGES_DEV * PAGE_TOKENS
    factor = HEAD_SIZE ** (-0.5)
    query_split_heads = query_rows.reshape(SELECTED_TOKENS, KEY_VALUE_HEADS, group_size, HEAD_SIZE)
    key_block_list = key_flattened.reshape(N_POS, block_index, KEY_VALUE_HEADS, HEAD_SIZE)
    value_block_list = value_flattened.reshape(N_POS, block_index, KEY_VALUE_HEADS, HEAD_SIZE)
    pos_blocks = key_pos.reshape(N_POS, block_index)
    results = []
    for head_index in range(KEY_VALUE_HEADS):
        head_query = query_split_heads[:, head_index].astype(jnp.float32)
        head_keys = key_block_list[:, :, head_index]
        head_values = value_block_list[:, :, head_index]

        def score_block(keys, places):
            scores = jnp.einsum('sgd,kd->sgk', head_query, keys.astype(jnp.float32)) * factor
            counted = places[None, None, :] <= selected_positions[:, None, None]
            return (scores, counted)

        def max_step(carry, item):
            scores, counted = score_block(item[0], item[1])
            return (jnp.maximum(carry, lax.optimization_barrier(jnp.max(jnp.where(counted, scores, -jnp.inf), axis=-1))), None)
        start = jnp.full((SELECTED_TOKENS, group_size), -jnp.inf, jnp.float32)
        top, _ = lax.scan(max_step, start, (head_keys, pos_blocks))

        def sum_step(carry, item):
            scores, counted = score_block(item[0], item[2])
            weights = jnp.where(counted, jnp.exp(scores - top[..., None]), 0.0)
            rounded = lax.optimization_barrier(weights.astype(jnp.bfloat16)).astype(jnp.float32)
            summed = jnp.einsum('sgk,kd->sgd', rounded, item[1].astype(jnp.float32))
            return ((carry[0] + lax.optimization_barrier(jnp.sum(weights, axis=-1)), carry[1] + summed), None)
        zeros = (jnp.zeros((SELECTED_TOKENS, group_size), jnp.float32), jnp.zeros((SELECTED_TOKENS, group_size, HEAD_SIZE), jnp.float32))
        (total, summed), _ = lax.scan(sum_step, zeros, (head_keys, head_values, pos_blocks))
        results.append(summed / total[..., None])
    blended = jnp.stack(results, axis=1).reshape(SELECTED_TOKENS, QUERY_HEADS * HEAD_SIZE).astype(jnp.bfloat16)
    return (blended, key_flattened.reshape(REQUEST_PAGES, PAGE_TOKENS, KEY_VALUE_HEADS * HEAD_SIZE), value_flattened.reshape(REQUEST_PAGES, PAGE_TOKENS, KEY_VALUE_HEADS * HEAD_SIZE))
```

```python
import functools

import jax
import jax.numpy as jnp
from jax import lax
from jax.experimental import pallas as pl
from jax.experimental.pallas import tpu as pltpu
from jax.sharding import Mesh, PartitionSpec as P

KEY_VALUE_HEADS = 4
GROUP = 8
W = 128
NY, NZ, NC = 4, 8, 2
ROWS = 256
OWN = 32
QCOLS = GROUP * W
COLS = QCOLS + 2 * W
EXTRA = 5 * W
STAT = 16
FAR_PAGE = 1024.0
LOWEST = -3.3e38
BF = jnp.bfloat16
F32 = jnp.float32
tie = lax.optimization_barrier
VMEM = pl.BlockSpec(memory_space=pltpu.VMEM)
ANY = pl.BlockSpec(memory_space=pl.ANY)
SMEM = pl.BlockSpec(memory_space=pltpu.SMEM)


def call(kernel, name, out_shape, specs, *operands, flops=0):
    return pl.pallas_call(
        kernel,
        grid=(1,),
        in_specs=specs,
        out_specs=jax.tree.map(lambda _: VMEM, out_shape),
        out_shape=out_shape,
        compiler_params=pltpu.CompilerParams(vmem_limit_bytes=56 * 1024 * 1024),
        cost_estimate=pl.CostEstimate(flops=flops, bytes_accessed=2_000_000, transcendentals=0),
        name=name,
    )(*operands)


def shaped(*shape, dtype=BF):
    return jax.ShapeDtypeStruct(shape, dtype)


def lanes(head):
    return pl.ds(pl.multiple_of(head * W, W), W)


def pass_kernel(*refs):
    pass


def pass_on(parts, flops):
    return pl.pallas_call(
        pass_kernel,
        in_specs=[ANY] * len(parts),
        out_specs=[ANY] * len(parts),
        out_shape=[shaped(*part.shape) for part in parts],
        input_output_aliases={i: i for i in range(len(parts))},
        cost_estimate=pl.CostEstimate(flops=flops, bytes_accessed=1_000, transcendentals=0),
        compiler_params=pltpu.CompilerParams(vmem_limit_bytes=56 * 1024 * 1024),
        name="pass_on",
    )(*parts)


def replaced_rows(pages_ref, selected):
    row = lax.broadcasted_iota(jnp.int32, (ROWS, 1), 0)
    page = jnp.where(row < W, pages_ref[0], pages_ref[1])
    pos = page * W + lax.rem(row, W)
    return jnp.max(jnp.where(pos == selected, 1.0, 0.0), axis=1, keepdims=True)


def replaced_rows(pages_ref, selected):
    row = lax.broadcasted_iota(jnp.int32, (ROWS, 1), 0)
    page = jnp.where(row < W, pages_ref[0], pages_ref[1])
    pos = page * W + lax.rem(row, W)
    return jnp.max(jnp.where(pos == selected, 1.0, 0.0), axis=1, keepdims=True)


def norm_kernel(hidden_ref, gain_ref, out_ref):
    values = hidden_ref[...].astype(F32)
    meansq = jnp.mean(values * values, axis=-1, keepdims=True)
    normed = (values * lax.rsqrt(meansq + 1e-05) * gain_ref[...].astype(F32)).astype(BF)
    for z in range(NZ):
        rows = jnp.concatenate([normed[:, (y * NZ + z) * NC * W : (y * NZ + z + 1) * NC * W] for y in range(NY)], 1)
        for y in range(NY):
            out_ref[y * NZ + z] = rows


def weights_kernel(place_ref, wq_ref, wk_ref, wv_ref, *out_refs):
    for s, out in enumerate(out_refs):
        head = lax.rem(place_ref[0] + s, NY)
        out[:, :QCOLS] = wq_ref[:, pl.ds(pl.multiple_of(head * QCOLS, QCOLS), QCOLS)]
        out[:, QCOLS : QCOLS + W] = wk_ref[:, lanes(head)]
        out[:, QCOLS + W :] = wv_ref[:, lanes(head)]


def blocks_kernel(place_ref, pages_ref, selected_ref, key_ref, value_ref, *out_refs):
    hit = jnp.broadcast_to(replaced_rows(pages_ref, selected_ref[...]), (ROWS, W))
    row = lax.broadcasted_iota(jnp.int32, (W, W), 0)
    meta = jnp.zeros((W, W), F32)
    for p in range(2):
        page = pages_ref[p].astype(F32)
        far = jnp.where(hit[p * W : (p + 1) * W].T[:1] > 0.5, FAR_PAGE, page)
        meta = jnp.where(row == p, far, jnp.where(row == 2 + p, page, meta))
    meta = meta.astype(BF)
    for s, out in enumerate(out_refs):
        at = lanes(lax.rem(place_ref[0] + s, NY))
        for p in range(2):
            out[:, p * W : (p + 1) * W] = key_ref[p, :, at]
            out[:, (2 + p) * W : (3 + p) * W] = value_ref[p, :, at]
        out[:, 4 * W :] = meta


def join_kernel(*refs):
    for s, part in enumerate(refs[:-1]):
        refs[-1][s * W : (s + 1) * W, :] = part[...]


def project_kernel(place_ref, normed_ref, *refs):
    weight_refs, out_ref = refs[:-1], refs[-1]
    y, c = place_ref[0], place_ref[1]
    parts = []
    for o in range(NC):
        core = c if o == 0 else 1 - c
        for s in range(NY):
            block = lax.rem(y + NY - s, NY) * NC + core
            parts.append(normed_ref[:, :, :, lanes(block)].astype(F32))
    rows = []
    for z in range(NZ):
        for u in range(NY):
            rows.append(jnp.concatenate([part[u, z] for part in parts], axis=1))
    left = jnp.concatenate(rows, axis=0).astype(BF)
    right = jnp.concatenate([ref[...] for ref in weight_refs], axis=0)
    out = jnp.dot(left, right, preferred_element_type=F32).astype(BF)
    for z in range(NZ):
        out_ref[z] = out[z * OWN : (z + 1) * OWN]


def rotate_kernel(partial_ref, cos_ref, sin_ref, out_ref, fresh_ref):
    def total(lo):
        value = partial_ref[0, :, lo : lo + W].astype(F32)
        for z in range(1, NZ):
            value += partial_ref[z, :, lo : lo + W].astype(F32)
        return value

    def rotated(value):
        return (value * cos_ref[...] + pltpu.roll(value, W // 2, 1) * sin_ref[...]).astype(BF)

    pieces = [rotated(total(head * W)) for head in range(GROUP + 1)] + [total(QCOLS + W).astype(BF)]
    for k, piece in enumerate(pieces):
        for a in range(NZ):
            out_ref[a, :, k * W : (k + 1) * W] = piece
    fresh_ref[:, :W] = pieces[GROUP]
    fresh_ref[:, W:] = pieces[GROUP + 1]


def score(query, keys):
    return lax.dot_general(query, keys, (((1,), (1,)), ((), ())), preferred_element_type=F32)


def attend_kernel(packed_ref, token_pos_ref, fresh_ref, fresh_c_ref, fresh_pos_ref, *refs):
    block_refs, out_ref = refs[:-1], refs[-1]
    factor = W**-0.5
    lane = lax.broadcasted_iota(jnp.int32, (1, W), 1).astype(F32)
    keys, values, pos = [], [], []
    for ref in block_refs:
        for s in range(NY):
            meta = ref[s * W : s * W + 16, 4 * W :].astype(F32)
            for p in range(2):
                keys.append(ref[s * W : (s + 1) * W, p * W : (p + 1) * W])
                values.append(ref[s * W : (s + 1) * W, (2 + p) * W : (3 + p) * W])
                pos.append(meta[p : p + 1] * W + lane)
    keys, values, pos = jnp.concatenate(keys, 0), jnp.concatenate(values, 0), jnp.concatenate(pos, 1)
    fresh = jnp.concatenate([fresh_ref[...], fresh_c_ref[...]], 0)
    count = NZ * OWN
    token_pos = jnp.concatenate([token_pos_ref[...]] * 2, 0)
    fresh_pos = fresh_pos_ref[...]

    def scores_of(pair):
        query = [packed_ref[a, :, h * W : (h + 1) * W] for h in (2 * pair, 2 * pair + 1) for a in range(NZ)]
        query = jnp.concatenate(query, 0)
        return score(query, keys), score(query, fresh[:, :W])

    stat_lane = lax.broadcasted_iota(jnp.int32, (count, W), 1)
    packed = jnp.zeros((count, W), F32)
    ahead = scores_of(0)
    for pair in range(GROUP // 2):
        now, now_fresh = ahead
        if pair + 1 < GROUP // 2:
            ahead = scores_of(pair + 1)
        now = jnp.where(pos <= token_pos, now * factor, -jnp.inf)
        now_fresh = jnp.where(fresh_pos <= token_pos, now_fresh * factor, -jnp.inf)
        top = jnp.maximum(jnp.max(now, axis=1, keepdims=True), jnp.max(now_fresh, axis=1, keepdims=True))
        top = jnp.maximum(top, LOWEST)
        weights, fresh_weights = jnp.exp(now - top), jnp.exp(now_fresh - top)
        total = jnp.sum(weights, axis=1, keepdims=True) + jnp.sum(fresh_weights, axis=1, keepdims=True)
        acc = jnp.dot(weights.astype(BF), values, preferred_element_type=F32)
        acc += jnp.dot(fresh_weights.astype(BF), fresh[:, W:], preferred_element_type=F32)
        some = total > 0.0
        safe = jnp.where(some, total, 1.0)
        result = acc * jnp.where(some, 1.0 / safe, 0.0)
        spread = jnp.where(some, top + jnp.log(safe), LOWEST)
        for k in range(2):
            head = 2 * pair + k
            packed = jnp.where(stat_lane // STAT == head, spread[k * count : (k + 1) * count], packed)
            for a in range(NZ):
                for u in range(NY):
                    at = k * count + (a * NY + u) * 8
                    out_ref[u * NZ + a, :, head * W : (head + 1) * W] = result[at : at + 8].astype(BF)
    high = packed.astype(BF).astype(F32)
    middle = (packed - high).astype(BF).astype(F32)
    which = lax.rem(stat_lane, STAT)
    packed = jnp.where(which == 0, high, jnp.where(which == 1, middle, packed - high - middle))
    for a in range(NZ):
        for u in range(NY):
            at = (a * NY + u) * 8
            out_ref[u * NZ + a, :, QCOLS:] = packed[at : at + 8].astype(BF)


def merge_kernel(parts_ref, out_ref):
    for u in range(NY):
        stats = [parts_ref[u * NZ + a, :, QCOLS:].astype(F32) for a in range(NZ)]
        spread = [s + pltpu.roll(s, W - 1, 1) + pltpu.roll(s, W - 2, 1) for s in stats]
        top = functools.reduce(jnp.maximum, spread)
        share = [jnp.exp(v - top) for v in spread]
        total = functools.reduce(jnp.add, share)
        share = [v / total for v in share]
        for head in range(GROUP):
            at = head * STAT
            value = jnp.zeros((8, W), F32)
            for a in range(NZ):
                value += share[a][:, at : at + 1] * parts_ref[u * NZ + a, :, head * W : (head + 1) * W].astype(F32)
            out_ref[:, u * QCOLS + head * W : u * QCOLS + (head + 1) * W] = value.astype(BF)


def place_kernel(packed_ref, other_ref, fresh_pos_ref, *refs):
    block_refs, out_refs = refs[:NY], refs[NY:]
    fresh = jnp.concatenate([ref[a, :, QCOLS:] for ref in (packed_ref, other_ref) for a in range(NZ)], 0)
    row = lax.broadcasted_iota(jnp.int32, (ROWS, 1), 0)
    offset = lax.rem(row, W).astype(F32)
    for block, out in zip(block_refs, out_refs):
        meta = block[:16, 4 * W :].astype(F32)
        pos = jnp.where(row < W, meta[2:3, :1], meta[3:4, :1]) * W + offset
        one_hot = jnp.where(pos == fresh_pos_ref[...], 1.0, 0.0).astype(BF)
        out[...] = jnp.dot(one_hot, fresh, preferred_element_type=F32).astype(BF)


def caches_kernel(place_ref, pages_ref, selected_ref, key_ref, value_ref, *refs):
    placed_refs, (new_key_ref, new_value_ref) = refs[:NY], refs[NY:]
    hit = replaced_rows(pages_ref, selected_ref[...]) > 0.5
    for s, placed in enumerate(placed_refs):
        at = lanes(lax.rem(place_ref[0] + s, NY))
        for p in range(2):
            rows = slice(p * W, (p + 1) * W)
            new_key_ref[p, :, at] = jnp.where(hit[rows], placed[rows, :W].astype(F32), key_ref[p, :, at].astype(F32)).astype(BF)
            new_value_ref[p, :, at] = jnp.where(hit[rows], placed[rows, W:].astype(F32), value_ref[p, :, at].astype(F32)).astype(BF)


def shift(values, axis, size, step):
    return lax.ppermute(values, axis, [(i, (i + step) % size) for i in range(size)])


def swap(values, axis):
    return shift(values, axis, 2, 1)


def exchange(values, axis):
    return lax.all_to_all(values, axis, split_axis=0, concat_axis=0, tiled=True)


def on_device(hidden, norm_gain, w_query, key_weight, value_weight, key_cache, value_cache, page_map, selected):
    y, z, c = (lax.axis_index(name) for name in ("y", "z", "c"))
    place = jnp.stack([y, c]).astype(jnp.int32)
    sel = selected.astype(F32).reshape(NY, NZ, NC, 8)
    selected_row = selected[None, :]

    sent = call(
        weights_kernel, "weights", [shaped(W, COLS)] * NY, [SMEM] + [VMEM] * 3, place, w_query, key_weight, value_weight
    )
    hidden, sent = tie((hidden, sent))
    w_own = [part if s == 0 else shift(part, "y", NY, s) for s, part in enumerate(sent)]

    normed = call(norm_kernel, "norm", shaped(NY * NZ, 8, NY * NC * W), [VMEM] * 2, hidden, norm_gain[None, :])
    normed, selected_row = tie((normed, selected_row))
    normed = exchange(normed, ("y", "z"))
    w_own = pass_on(w_own, 40_000_000_000)
    w_other = [swap(part, "c") for part in w_own]

    blocks = call(
        blocks_kernel,
        "blocks",
        [shaped(W, EXTRA)] * NY,
        [SMEM, SMEM] + [VMEM] * 3,
        place,
        page_map,
        selected_row,
        key_cache,
        value_cache,
    )
    blocks = [part if s == 0 else shift(part, "y", NY, s) for s, part in enumerate(blocks)]
    mine = call(join_kernel, "join", shaped(NY * W, EXTRA), [VMEM] * NY, *blocks)

    partial = call(
        project_kernel,
        "project",
        shaped(NZ, OWN, COLS),
        [SMEM] + [VMEM] * 9,
        place,
        normed.reshape(NY, NZ, 8, -1),
        *w_own,
        *w_other,
        flops=700_000_000,
    )
    partial = exchange(partial, "z")
    cached = [mine, swap(mine, "c")]

    group = lambda core: lax.dynamic_index_in_dim(sel, core, 2, keepdims=False).transpose(1, 0, 2).reshape(NZ, OWN)
    groups = [group(c), group(1 - c)]
    here = lambda pos: lax.dynamic_index_in_dim(pos, z, 0, keepdims=False)
    half = W // 2
    frequency = 500000.0 ** (-(jnp.arange(half, dtype=F32) * 2.0 / W))
    angles = here(groups[0])[:, None] * frequency[None, :]
    cosine, sine = jnp.cos(angles), jnp.sin(angles)
    packed, fresh = call(
        rotate_kernel,
        "rotate",
        [shaped(NZ, OWN, COLS), shaped(OWN, 2 * W)],
        [VMEM] * 3,
        partial,
        jnp.concatenate([cosine, cosine], 1),
        jnp.concatenate([-sine, sine], 1),
    )
    packed = exchange(packed, "z")

    parts = call(
        attend_kernel,
        "attend",
        shaped(NY * NZ, 8, QCOLS + W),
        [VMEM] * 7,
        packed,
        groups[0].reshape(-1, 1),
        fresh,
        swap(fresh, "c"),
        jnp.concatenate([here(g) for g in groups])[None, :],
        *cached,
        flops=2_200_000_000,
    )
    parts = exchange(parts, ("y", "z"))
    blended = call(merge_kernel, "merge", shaped(8, NY * QCOLS), [VMEM], parts)

    placed = call(
        place_kernel,
        "place",
        [shaped(ROWS, 2 * W)] * NY,
        [VMEM] * 7,
        packed,
        swap(packed, "c"),
        jnp.concatenate([g.reshape(-1) for g in groups])[None, :],
        *blocks,
    )
    placed = [part if s == 0 else shift(part, "y", NY, NY - s) for s, part in enumerate(placed)]
    new_key, new_value = call(
        caches_kernel,
        "caches",
        [shaped(2, W, KEY_VALUE_HEADS * W)] * 2,
        [SMEM, SMEM] + [VMEM] * 7,
        place,
        page_map,
        selected_row,
        key_cache,
        value_cache,
        *placed,
    )
    return blended, new_key, new_value


def solution(mesh):
    fine = Mesh(mesh.devices.reshape(mesh.devices.shape[0], NY, NZ, NC), ("req", "y", "z", "c"))
    every = ("req", "y", "z", "c")
    pos = every[1:]
    return jax.shard_map(
        on_device,
        mesh=fine,
        in_specs=(
            P(every, None),
            P(),
            P(pos, None),
            P(pos, None),
            P(pos, None),
            P(every, None, None),
            P(every, None, None),
            P(every),
            P("req"),
        ),
        out_specs=(P(every, None), P(every, None, None), P(every, None, None)),
        check_vma=False,
    )
```
